32 devices in a mesh: groups: 2 (over y), replica: 8 (over z, x), tensor: 2 (over core).
Axes of the slice: x: 2, y: 2, z: 4, core: 2. Of those that a mesh axis runs over, the one named last changes fastest.
Arguments:
- queries: bfloat16 [32, 4096], P(('groups', 'replica'), 'tensor'), parts along dimension 0
- new_keys: bfloat16 [32, 512], P(('groups', 'replica'), 'tensor'), parts along dimension 0, may hold values from -6 to 6
- new_values: bfloat16 [32, 512], P(('groups', 'replica'), 'tensor'), parts along dimension 0, may hold values from -6 to 6
- key_cache: bfloat16 [32, 1024, 512], P(('groups', 'replica'), None, 'tensor'), parts along dimension 0
- value_cache: bfloat16 [32, 1024, 512], P(('groups', 'replica'), None, 'tensor'), parts along dimension 0, may hold values from -6 to 6
- lengths: int32 [32], P(('groups', 'replica')), parts along dimension 0, may hold values from 2 to 1024, as said below
- base_held: bfloat16 [5120, 512], P('replica', 'tensor'), may hold values from -0.078125 to 0.078125
- adapter_a: bfloat16 [5120, 16], P('replica'), may hold values from -6 to 6
- adapter_b: bfloat16 [16, 512], P(None, 'tensor'), may hold values from -0.01953125 to 0.01953125
- owners: int32 [8], replicated, may hold values from 0 to 7, each once
Outputs:
- handed_rows: bfloat16 [32, 4096], P(('groups', 'replica'), 'tensor'), parts along dimension 0
- block_values: bfloat16 [10240, 512], P('groups', 'tensor'), parts along dimension 0
- block_scales: float32 [80, 4], P('groups', 'tensor'), parts along dimension 0
The draws below stay inside these ranges and needn't reach their ends.
There are 2 independent parts, one for each index of `groups`. The reference program is written for one: setup_inputs(seed, part) draws one part's arguments, and reference() takes and returns one part's arrays. A program takes and returns all parts, laid end to end along the dimension named above; an argument that names none is the same for every part. Nothing has to cross between parts.
Inputs may be any that keep to these rules, and one draw needn't show every extreme that they name: Some row has lengths equal to 1024.
All inputs are finite; a program needn't handle non-finite values. Where the reference program divides by a largest or mean magnitude, that divisor is 1e-20 or more.
Results may differ from the reference program's by a relative error of at most 0.0059.
Values may be sent and summed in bfloat16 or wider, within the bound.
A program may use at most 64 MiB of HBM per device.

```python
import jax
import jax.numpy as jnp
from jax import lax

D = 5120
HD = 128
QHEADS = 32
KVHEADS = 4
RANK = 16
BLOCK = 128
ROWS_DEV = 2
CACHE = 1024
ROWS = 16
COLS = 512
N_REPLICA = 8


def cache_normals(key):
    return jax.random.normal(jax.random.fold_in(key, 17), (ROWS, CACHE, COLS), jnp.float32)


def draw_key_cache(key, part):
    cached = cache_normals(key)
    return cached.astype(jnp.bfloat16)


def draw_queries(key, part):
    key = jax.random.fold_in(key, 5)
    drawn = jax.random.normal(key, (ROWS, QHEADS * HD), jnp.float32)
    return drawn.astype(jnp.bfloat16)


def draw_lengths(key, part):
    key = jax.random.fold_in(key, 7)
    key_one, key_two = jax.random.split(key)
    filled = jax.random.randint(key_one, (ROWS,), 2, CACHE + 1)
    longest = jax.random.randint(key_two, (), 0, ROWS)
    return jnp.where(jnp.arange(ROWS) == longest, CACHE, filled).astype(jnp.int32)


def shard_levels(key, extent, pieces, least, high):
    gain, own = 1.0, jax.random.fold_in(key, 6)
    for position, blocks in pieces:
        steps = jnp.exp(jax.random.uniform(jax.random.fold_in(own, position), (blocks,), jnp.float32, least / len(pieces), high / len(pieces)))
        gain = gain * jnp.repeat(steps, extent[position] // blocks).reshape([-1 if axis == position else 1 for axis in range(len(extent))])
    return gain


def gaussian(stream_key, extent, width, most, pieces=(), dtype=jnp.bfloat16):
    values = jax.random.normal(stream_key, extent, jnp.float32) * width
    if len(pieces) > 0:
        values = shard_levels(stream_key, extent, pieces, -0.22, 0.18) * values
    return jnp.clip(values, min=-most, max=most).astype(dtype)


def setup_inputs(seed: int = 0, part: int = 0) -> dict:
    splits = jax.random.split(jax.random.key(seed), 11)
    own_keys = jax.random.split(jax.random.fold_in(splits[10], part), 11)
    queries = draw_queries(jax.random.fold_in(jax.random.fold_in(splits[10], part), 71), part)
    new_keys = gaussian(own_keys[1], (ROWS, COLS), 1.0, 6.0, ((0, 8), (1, 2)))
    new_values = gaussian(own_keys[2], (ROWS, COLS), 1.0, 6.0, ((0, 8), (1, 2)))
    key_cache = draw_key_cache(jax.random.fold_in(jax.random.fold_in(splits[10], part), 71), part)
    value_cache = gaussian(own_keys[4], (ROWS, CACHE, COLS), 1.0, 6.0, ((0, 8), (2, 2)))
    lengths = draw_lengths(jax.random.fold_in(jax.random.fold_in(splits[10], part), 71), part)
    base_held = gaussian(splits[6], (D, COLS), D ** -0.5, 0.078125, ((0, 8), (1, 2)))
    adapter_a = gaussian(splits[7], (D, RANK), 1.0, 6.0, ((0, 8),))
    adapter_b = gaussian(splits[8], (RANK, COLS), (RANK * D) ** -0.5, 0.01953125, ((1, 2),))
    owners = jax.random.permutation(splits[9], N_REPLICA).astype(jnp.int32)
    return {"queries": queries, "new_keys": new_keys, "new_values": new_values, "key_cache": key_cache, "value_cache": value_cache, "lengths": lengths, "base_held": base_held, "adapter_a": adapter_a, "adapter_b": adapter_b, "owners": owners}


def attend_row(packed):
    query_row, key_new, value_new, key_rows, value_rows, filled = packed
    per_group = QHEADS // KVHEADS
    scaling = 1.0 / (HD ** 0.5)
    query_heads = query_row.astype(jnp.float32).reshape(KVHEADS, per_group, HD)
    cached_keys = key_rows.astype(jnp.float32).reshape(CACHE, KVHEADS, HD)
    cached_values = value_rows.astype(jnp.float32).reshape(CACHE, KVHEADS, HD)
    scores = jnp.einsum('gqd,lgd->gql', query_heads, cached_keys) * scaling
    usable = jnp.arange(CACHE) < filled
    scores = jnp.where(usable[None, None, :], scores, -jnp.inf)
    own_score = jnp.einsum('gqd,gd->gq', query_heads, key_new.astype(jnp.float32).reshape(KVHEADS, HD)) * scaling
    highest = jnp.maximum(jnp.max(scores, axis=-1), own_score)
    raised = jnp.exp(scores - highest[..., None])
    own_raised = jnp.exp(own_score - highest)
    totals = jnp.sum(raised, axis=-1) + own_raised
    weights = (raised / totals[..., None]).astype(jnp.bfloat16)
    own_weight = (own_raised / totals).astype(jnp.bfloat16)
    mixed = jnp.einsum('gql,lgd->gqd', weights.astype(jnp.float32), cached_values)
    mixed = mixed + own_weight.astype(jnp.float32)[..., None] * value_new.astype(jnp.float32).reshape(KVHEADS, 1, HD)
    return mixed.reshape(QHEADS * HD).astype(jnp.bfloat16)


def reference(queries, new_keys, new_values, key_cache, value_cache, lengths, base_held, adapter_a, adapter_b, owners):
    merged_held = (base_held.astype(jnp.float32) + jnp.dot(adapter_a, adapter_b, preferred_element_type=jnp.float32)).astype(jnp.bfloat16)
    slice_rows = D // N_REPLICA
    assembled = merged_held.reshape(N_REPLICA, slice_rows, COLS)[owners].reshape(D, COLS)
    tiled = assembled.astype(jnp.float32).reshape(D // BLOCK, BLOCK, COLS // BLOCK, BLOCK)
    block_scales = jnp.max(jnp.abs(tiled), axis=(1, 3)) + 1e-6
    block_values = (tiled / block_scales[:, None, :, None]).reshape(D, COLS).astype(jnp.bfloat16)
    attended = lax.map(attend_row, (queries, new_keys, new_values, key_cache, value_cache, lengths))
    handed_rows = jnp.roll(attended.reshape(N_REPLICA, ROWS_DEV, QHEADS * HD), 1, axis=0).reshape(ROWS, QHEADS * HD)
    return handed_rows, block_values, block_scales
```

```python
import jax
import jax.numpy as jnp
from jax import lax
from jax.experimental import pallas as pl
from jax.experimental.pallas import tpu as pltpu
from jax.sharding import PartitionSpec as P

HD = 128
BLOCK = 128


def from_behind(value, axis, steps):
    count = lax.axis_size(axis)
    pairs = [(source, (source + steps) % count) for source in range(count)]
    return lax.ppermute(value, axis, pairs)


def merge_rows(base_rows, factor_rows, adapter_b):
    return (
        base_rows.astype(jnp.float32)
        + jnp.dot(factor_rows, adapter_b, preferred_element_type=jnp.float32)
    ).astype(jnp.bfloat16)


def on_device(
    queries,
    new_keys,
    new_values,
    key_cache,
    value_cache,
    lengths,
    base_held,
    adapter_a,
    adapter_b,
    owners,
):
    replicas = lax.axis_size("replica")
    slice_rows, columns = base_held.shape
    merged = merge_rows(base_held, adapter_a, adapter_b)
    everything = lax.all_gather(merged, "replica", axis=0, tiled=True)
    assembled = jnp.take(everything.reshape(replicas, slice_rows, columns), owners, axis=0).reshape(
        replicas * slice_rows, columns
    )
    total_rows = assembled.shape[0]
    tiled = assembled.astype(jnp.float32).reshape(
        total_rows // BLOCK, BLOCK, columns // BLOCK, BLOCK
    )
    block_scales = jnp.max(jnp.abs(tiled), axis=(1, 3)) + 1e-06
    block_values = (
        (tiled / block_scales[:, None, :, None]).reshape(total_rows, columns).astype(jnp.bfloat16)
    )
    row_count = queries.shape[0]
    slot_count = key_cache.shape[1]
    kv_heads = key_cache.shape[2] // HD
    per_group = queries.shape[1] // HD // kv_heads
    scaling = 1.0 / HD**0.5
    query_heads = queries.reshape(row_count, kv_heads, per_group, HD)
    cached_keys = key_cache.reshape(row_count, slot_count, kv_heads, HD)
    cached_values = value_cache.reshape(row_count, slot_count, kv_heads, HD)
    scores = (
        jnp.einsum("rgqd,rlgd->rgql", query_heads, cached_keys, preferred_element_type=jnp.float32)
        * scaling
    )
    usable = jnp.arange(slot_count)[None, None, None, :] < lengths[:, None, None, None]
    scores = jnp.where(usable, scores, -jnp.inf)
    own_score = (
        jnp.einsum(
            "rgqd,rgd->rgq",
            query_heads,
            new_keys.reshape(row_count, kv_heads, HD),
            preferred_element_type=jnp.float32,
        )
        * scaling
    )
    highest = jnp.maximum(jnp.max(scores, axis=-1), own_score)
    raised = jnp.exp(scores - highest[..., None])
    own_raised = jnp.exp(own_score - highest)
    totals = jnp.sum(raised, axis=-1) + own_raised
    weights = (raised / totals[..., None]).astype(jnp.bfloat16)
    own_weight = (own_raised / totals).astype(jnp.bfloat16)
    mixed = jnp.einsum(
        "rgql,rlgd->rgqd", weights, cached_values, preferred_element_type=jnp.float32
    )
    mixed = mixed + own_weight.astype(jnp.float32)[..., None] * new_values.reshape(
        row_count, kv_heads, 1, HD
    ).astype(jnp.float32)
    attended = mixed.reshape(row_count, kv_heads * per_group * HD).astype(jnp.bfloat16)
    handed_rows = from_behind(attended, "replica", 1)
    return (handed_rows, block_values, block_scales)


def sixteen(rows):
    return max(16, rows // 16 * 16)


def gather_kernel(
    queries_ref,
    new_keys_ref,
    new_values_ref,
    lengths_ref,
    base_ref,
    factor_ref,
    adapter_b_ref,
    keys_hbm,
    values_hbm,
    gathered,
    scales_all,
    handed,
    own,
    own_scales,
    attended,
    keys,
    values,
    local_sem,
    z_send,
    z_recv,
    x_send,
    x_recv,
    y_send,
    y_recv,
    scale_send,
    scale_recv,
    hand_sem,
):
    group = lax.axis_index("groups")
    me = lax.axis_index("replica")
    count = lax.axis_size("replica")
    depth = count // 2
    z = me // 2
    x = me % 2
    rows, columns = base_ref.shape
    row_count, slot_count, _ = keys.shape
    kv_heads = columns // HD
    per_group = queries_ref.shape[1] // HD // kv_heads

    keys_in = pltpu.make_async_copy(keys_hbm, keys, local_sem.at[0])
    values_in = pltpu.make_async_copy(values_hbm, values, local_sem.at[1])
    keys_in.start()
    values_in.start()

    barrier = pltpu.get_barrier_semaphore()
    for step in range(1, count):
        pl.semaphore_signal(
            barrier, inc=1, device_id={"replica": lax.rem(me + step, count)}
        )
    pl.semaphore_signal(barrier, inc=1, device_id={"groups": 1 - group})

    lane = lax.broadcasted_iota(jnp.int32, own_scales.shape, 1)
    line = lax.broadcasted_iota(jnp.int32, own_scales.shape, 0)
    blocks = rows // BLOCK
    spread = jnp.zeros(own_scales.shape, jnp.float32)
    for block in range(blocks):
        part = pl.ds(block * BLOCK, BLOCK)
        product = lax.dot_general(
            factor_ref[:, block * BLOCK : (block + 1) * BLOCK],
            adapter_b_ref[...],
            (((0,), (0,)), ((), ())),
            preferred_element_type=jnp.float32,
        )
        merged = (base_ref[part, :].astype(jnp.float32) + product).astype(jnp.bfloat16)
        for column in range(columns // BLOCK):
            tile = merged[:, column * BLOCK : (column + 1) * BLOCK].astype(jnp.float32)
            scale = jnp.max(jnp.abs(tile), axis=(0, 1), keepdims=True) + 1e-06
            own[part, column * BLOCK : (column + 1) * BLOCK] = (tile / scale).astype(jnp.bfloat16)
            spread = jnp.where((lane % blocks == block) & (line == column), scale, spread)
    own_scales[...] = spread

    pl.semaphore_wait(barrier, count)

    z_end, x_end = sixteen(rows * 31 // 40), sixteen(rows * 3 // 5)
    cut = sixteen(rows * 2 // 5)
    z_pieces = ((0, cut), (cut, z_end))
    x_pieces = ((0, cut), (cut, x_end))
    yx_piece, yz_piece = (0, rows - x_end), (0, rows - z_end)

    def window(ref, piece, side):
        low, high = piece
        start = pl.multiple_of(low + side * (rows - high - low), 16)
        return ref.at[pl.ds(start, high - low)]

    def copy(source, plane, column, piece, side, send, recv, device):
        target = gathered.at[plane * 2 + column]
        source = target if source is None else source
        return pltpu.make_async_remote_copy(
            src_ref=window(source, piece, side),
            dst_ref=window(target, piece, side),
            send_sem=send,
            recv_sem=recv,
            device_id=device,
        )

    def z_copy(plane, piece, way, source=None):
        return copy(
            source,
            plane,
            x,
            z_pieces[piece],
            group,
            z_send.at[(way + 1) // 2, plane, piece],
            z_recv.at[plane, piece],
            {"replica": lax.rem(me + 2 * way + count, count)},
        )

    def x_copy(plane, piece, column, source=None):
        return copy(
            source,
            plane,
            column,
            x_pieces[piece],
            group,
            x_send.at[plane, piece],
            x_recv.at[plane, piece],
            {"replica": z * 2 + 1 - x},
        )

    def y_copy(plane, column, which, side):
        return copy(
            None,
            plane,
            column,
            (yx_piece, yz_piece)[which],
            side,
            y_send.at[which, plane],
            y_recv.at[which, plane],
            {"groups": 1 - group},
        )

    def scale_copy(step):
        return pltpu.make_async_remote_copy(
            src_ref=own_scales,
            dst_ref=scales_all.at[me],
            send_sem=scale_send.at[step],
            recv_sem=scale_recv.at[step],
            device_id={"replica": lax.rem(me + step, count)},
        )

    def attend(row, head):
        first = head * per_group
        query = jnp.concatenate(
            [
                queries_ref[row : row + 1, (first + i) * HD : (first + i + 1) * HD].astype(
                    jnp.float32
                )
                for i in range(per_group)
            ],
            axis=0,
        )
        wide = slice(head * HD, (head + 1) * HD)
        scaling = 1.0 / HD**0.5
        scores = (
            lax.dot_general(
                query.astype(jnp.bfloat16),
                keys[row, :, wide],
                (((1,), (1,)), ((), ())),
                preferred_element_type=jnp.float32,
            )
            * scaling
        )
        slot = lax.broadcasted_iota(jnp.int32, scores.shape, 1)
        scores = jnp.where(slot < lengths_ref[row], scores, -jnp.inf)
        new_key = new_keys_ref[row : row + 1, wide].astype(jnp.float32)
        own_score = jnp.sum(query * new_key, axis=1, keepdims=True) * scaling
        highest = jnp.maximum(jnp.max(scores, axis=1, keepdims=True), own_score)
        raised = jnp.exp(scores - highest)
        own_raised = jnp.exp(own_score - highest)
        totals = jnp.sum(raised, axis=1, keepdims=True) + own_raised
        weights = (raised / totals).astype(jnp.bfloat16)
        own_weight = (own_raised / totals).astype(jnp.bfloat16).astype(jnp.float32)
        mixed = jnp.dot(weights, values[row, :, wide], preferred_element_type=jnp.float32)
        new_value = new_values_ref[row : row + 1, wide].astype(jnp.float32)
        return mixed + own_weight * new_value

    for piece in range(2):

        @pl.when(z < depth - 1)
        def _():
            z_copy(z, piece, 1, own).start()

        @pl.when(z > 0)
        def _():
            z_copy(z, piece, -1, own).start()

        x_copy(z, piece, x, own).start()
    for step in range(1, count):
        scale_copy(step).start()
    own_out = pltpu.make_async_copy(own, gathered.at[me], local_sem.at[2])
    own_out.start()
    scales_out = pltpu.make_async_copy(own_scales, scales_all.at[me], local_sem.at[3])
    scales_out.start()

    def z_step(plane, piece, way):
        z_copy(plane, piece, way).wait_recv()

        @pl.when((z + way >= 0) & (z + way < depth))
        def _():
            z_copy(plane, piece, way).start()

        x_copy(plane, piece, x).start()
        if piece == 0:
            y_copy(plane, x, 1, group).start()

    def x_step(plane, piece):
        x_copy(plane, piece, 1 - x).wait_recv()
        if piece == 0:
            y_copy(plane, 1 - x, 0, group).start()

    keys_in.wait()
    values_in.wait()
    units = [(row, head) for row in range(row_count) for head in range(kv_heads)]
    done = [attend(*unit) for unit in units]
    tall = jnp.concatenate(done, axis=0)
    attended[...] = tall.astype(jnp.bfloat16)
    hand = pltpu.make_async_remote_copy(
        src_ref=attended,
        dst_ref=handed,
        send_sem=hand_sem.at[0],
        recv_sem=hand_sem.at[1],
        device_id={"replica": lax.rem(me + 1, count)},
    )
    hand.start()

    for step in range(1, depth + 1):
        for piece in range(2):
            if step < depth:

                @pl.when(z - step >= 0)
                def _():
                    z_step(z - step, piece, 1)

                @pl.when(z + step < depth)
                def _():
                    z_step(z + step, piece, -1)

            if step == 1:
                x_step(z, piece)
            else:

                @pl.when(z - step + 1 >= 0)
                def _():
                    x_step(z - step + 1, piece)

                @pl.when(z + step - 1 < depth)
                def _():
                    x_step(z + step - 1, piece)

    own_out.wait()
    scales_out.wait()
    hand.wait()
    for step in range(1, count):
        scale_copy(step).wait()
    for plane in range(depth):
        for piece in range(2):

            @pl.when((plane <= z) & (z < depth - 1))
            def _():
                z_copy(plane, piece, 1).wait_send()

            @pl.when((plane >= z) & (z > 0))
            def _():
                z_copy(plane, piece, -1).wait_send()

            x_copy(plane, piece, x).wait_send()
        y_copy(plane, 1 - x, 0, group).wait_send()
        y_copy(plane, 1 - x, 0, 1 - group).wait_recv()

        @pl.when(z != plane)
        def _():
            y_copy(plane, x, 1, group).wait_send()
            y_copy(plane, x, 1, 1 - group).wait_recv()


def place_kernel(owners_ref, scales_ref, handed_ref, gathered, placed, scales, rows_out, sems):
    count, rows, _ = gathered.shape
    copies = [
        pltpu.make_async_copy(
            gathered.at[owners_ref[slot]], placed.at[pl.ds(slot * rows, rows)], sems.at[slot]
        )
        for slot in range(count)
    ]
    for moving in copies:
        moving.start()
    blocks = scales.shape[1] // count
    lane = lax.broadcasted_iota(jnp.int32, scales_ref.shape[1:], 1)
    spread = jnp.zeros(scales_ref.shape[1:], jnp.float32)
    for slot in range(count):
        spread = jnp.where(lane // blocks == slot, scales_ref[owners_ref[slot]], spread)
    scales[...] = spread[: scales.shape[0], : scales.shape[1]]
    tall = handed_ref[...].astype(jnp.float32)
    row_count = rows_out.shape[0]
    heads = tall.shape[0] // row_count
    for row in range(row_count):
        rows_out[row : row + 1, :] = jnp.concatenate(
            [tall[row * heads + head : row * heads + head + 1] for head in range(heads)], axis=1
        ).astype(jnp.bfloat16)
    for moving in copies:
        moving.wait()


def on_plane(
    queries,
    new_keys,
    new_values,
    key_cache,
    value_cache,
    lengths,
    base_held,
    adapter_a,
    adapter_b,
    owners,
):
    replicas = lax.axis_size("replica")
    depth = replicas // 2
    rows, columns = base_held.shape
    row_count = queries.shape[0]
    heads = row_count * queries.shape[1] // HD
    vmem = pl.BlockSpec(memory_space=pltpu.VMEM)
    smem = pl.BlockSpec(memory_space=pltpu.SMEM)
    anywhere = pl.BlockSpec(memory_space=pl.ANY)
    gathered, scales_all, handed = pl.pallas_call(
        gather_kernel,
        out_shape=(
            jax.ShapeDtypeStruct((replicas, rows, columns), jnp.bfloat16),
            jax.ShapeDtypeStruct((replicas, 8, 128), jnp.float32),
            jax.ShapeDtypeStruct((heads, HD), jnp.bfloat16),
        ),
        in_specs=[vmem, vmem, vmem, smem, vmem, vmem, vmem, anywhere, anywhere],
        out_specs=(anywhere, anywhere, anywhere),
        scratch_shapes=[
            pltpu.VMEM((rows, columns), jnp.bfloat16),
            pltpu.VMEM((8, 128), jnp.float32),
            pltpu.VMEM((heads, HD), jnp.bfloat16),
            pltpu.VMEM(key_cache.shape, jnp.bfloat16),
            pltpu.VMEM(value_cache.shape, jnp.bfloat16),
            pltpu.SemaphoreType.DMA((4,)),
            pltpu.SemaphoreType.DMA((2, depth, 2)),
            pltpu.SemaphoreType.DMA((depth, 2)),
            pltpu.SemaphoreType.DMA((depth, 2)),
            pltpu.SemaphoreType.DMA((depth, 2)),
            pltpu.SemaphoreType.DMA((2, depth)),
            pltpu.SemaphoreType.DMA((2, depth)),
            pltpu.SemaphoreType.DMA((replicas,)),
            pltpu.SemaphoreType.DMA((replicas,)),
            pltpu.SemaphoreType.DMA((2,)),
        ],
        compiler_params=pltpu.CompilerParams(
            collective_id=0, has_side_effects=True, vmem_limit_bytes=24 * 2**20
        ),
        name="gather",
    )(
        queries,
        new_keys,
        new_values,
        lengths,
        base_held,
        adapter_a.T,
        adapter_b,
        key_cache,
        value_cache,
    )
    block_values, scales, handed_rows = pl.pallas_call(
        place_kernel,
        out_shape=(
            jax.ShapeDtypeStruct((replicas * rows, columns), jnp.bfloat16),
            jax.ShapeDtypeStruct((columns // BLOCK, replicas * rows // BLOCK), jnp.float32),
            jax.ShapeDtypeStruct(queries.shape, jnp.bfloat16),
        ),
        in_specs=[smem, vmem, vmem, anywhere],
        out_specs=(anywhere, vmem, vmem),
        scratch_shapes=[pltpu.SemaphoreType.DMA((replicas,))],
        name="place",
    )(owners, scales_all, handed, gathered)
    return (handed_rows, block_values, scales.T)


def solution(mesh):
    shape = dict(mesh.shape)
    relay = shape["groups"] == 2 and shape["replica"] % 2 == 0

    def either(*operands):
        rows, columns = operands[6].shape
        blocks = shape["replica"] * rows // BLOCK
        if relay and shape["replica"] <= 16 and rows % BLOCK == 0 and blocks <= 128 and columns <= 8 * BLOCK:
            return on_plane(*operands)
        return on_device(*operands)

    in_specs = (
        P(("groups", "replica"), "tensor"),
        P(("groups", "replica"), "tensor"),
        P(("groups", "replica"), "tensor"),
        P(("groups", "replica"), None, "tensor"),
        P(("groups", "replica"), None, "tensor"),
        P(("groups", "replica")),
        P("replica", "tensor"),
        P("replica", None),
        P(None, "tensor"),
        P(),
    )
    out_specs = (P(("groups", "replica"), "tensor"), P("groups", "tensor"), P("groups", "tensor"))
    return jax.shard_map(
        either, mesh=mesh, in_specs=in_specs, out_specs=out_specs, check_vma=False
    )
```

```python
import jax
import jax.numpy as jnp
from jax import lax
from jax.experimental import pallas as pl
from jax.experimental.pallas import tpu as pltpu
from jax.sharding import PartitionSpec as P

HD = 128
BLOCK = 128


def from_behind(value, axis, steps):
    count = lax.axis_size(axis)
    pairs = [(source, (source + steps) % count) for source in range(count)]
    return lax.ppermute(value, axis, pairs)


def merge_rows(base_rows, factor_rows, adapter_b):
    return (
        base_rows.astype(jnp.float32)
        + jnp.dot(factor_rows, adapter_b, preferred_element_type=jnp.float32)
    ).astype(jnp.bfloat16)


def on_device(
    queries,
    new_keys,
    new_values,
    key_cache,
    value_cache,
    lengths,
    base_held,
    adapter_a,
    adapter_b,
    owners,
):
    replicas = lax.axis_size("replica")
    slice_rows, columns = base_held.shape
    merged = merge_rows(base_held, adapter_a, adapter_b)
    everything = lax.all_gather(merged, "replica", axis=0, tiled=True)
    assembled = jnp.take(everything.reshape(replicas, slice_rows, columns), owners, axis=0).reshape(
        replicas * slice_rows, columns
    )
    total_rows = assembled.shape[0]
    tiled = assembled.astype(jnp.float32).reshape(
        total_rows // BLOCK, BLOCK, columns // BLOCK, BLOCK
    )
    block_scales = jnp.max(jnp.abs(tiled), axis=(1, 3)) + 1e-06
    block_values = (
        (tiled / block_scales[:, None, :, None]).reshape(total_rows, columns).astype(jnp.bfloat16)
    )
    row_count = queries.shape[0]
    slot_count = key_cache.shape[1]
    kv_heads = key_cache.shape[2] // HD
    per_group = queries.shape[1] // HD // kv_heads
    scaling = 1.0 / HD**0.5
    query_heads = queries.reshape(row_count, kv_heads, per_group, HD)
    cached_keys = key_cache.reshape(row_count, slot_count, kv_heads, HD)
    cached_values = value_cache.reshape(row_count, slot_count, kv_heads, HD)
    scores = (
        jnp.einsum("rgqd,rlgd->rgql", query_heads, cached_keys, preferred_element_type=jnp.float32)
        * scaling
    )
    usable = jnp.arange(slot_count)[None, None, None, :] < lengths[:, None, None, None]
    scores = jnp.where(usable, scores, -jnp.inf)
    own_score = (
        jnp.einsum(
            "rgqd,rgd->rgq",
            query_heads,
            new_keys.reshape(row_count, kv_heads, HD),
            preferred_element_type=jnp.float32,
        )
        * scaling
    )
    highest = jnp.maximum(jnp.max(scores, axis=-1), own_score)
    raised = jnp.exp(scores - highest[..., None])
    own_raised = jnp.exp(own_score - highest)
    totals = jnp.sum(raised, axis=-1) + own_raised
    weights = (raised / totals[..., None]).astype(jnp.bfloat16)
    own_weight = (own_raised / totals).astype(jnp.bfloat16)
    mixed = jnp.einsum(
        "rgql,rlgd->rgqd", weights, cached_values, preferred_element_type=jnp.float32
    )
    mixed = mixed + own_weight.astype(jnp.float32)[..., None] * new_values.reshape(
        row_count, kv_heads, 1, HD
    ).astype(jnp.float32)
    attended = mixed.reshape(row_count, kv_heads * per_group * HD).astype(jnp.bfloat16)
    handed_rows = from_behind(attended, "replica", 1)
    return (handed_rows, block_values, block_scales)


def sixteen(rows):
    return max(16, rows // 16 * 16)


def gather_kernel(
    queries_ref,
    new_keys_ref,
    new_values_ref,
    lengths_ref,
    base_ref,
    factor_ref,
    adapter_b_ref,
    keys_hbm,
    values_hbm,
    gathered,
    scales_all,
    handed,
    own,
    own_scales,
    attended,
    keys,
    values,
    local_sem,
    z_send,
    z_recv,
    x_send,
    x_recv,
    y_send,
    y_recv,
    scale_send,
    scale_recv,
    hand_sem,
):
    group = lax.axis_index("groups")
    me = lax.axis_index("replica")
    count = lax.axis_size("replica")
    depth = count // 2
    z = me // 2
    x = me % 2
    rows, columns = base_ref.shape
    row_count, slot_count, _ = keys.shape
    kv_heads = columns // HD
    per_group = queries_ref.shape[1] // HD // kv_heads

    keys_in = pltpu.make_async_copy(keys_hbm, keys, local_sem.at[0])
    values_in = pltpu.make_async_copy(values_hbm, values, local_sem.at[1])
    keys_in.start()
    values_in.start()

    barrier = pltpu.get_barrier_semaphore()
    for step in range(1, count):
        pl.semaphore_signal(
            barrier, inc=1, device_id={"replica": lax.rem(me + step, count)}
        )
    pl.semaphore_signal(barrier, inc=1, device_id={"groups": 1 - group})

    lane = lax.broadcasted_iota(jnp.int32, own_scales.shape, 1)
    line = lax.broadcasted_iota(jnp.int32, own_scales.shape, 0)
    blocks = rows // BLOCK

    def scale_block(step, spread):
        block = step + group * (blocks - 1 - 2 * step)
        part = pl.ds(pl.multiple_of(block * BLOCK, BLOCK), BLOCK)
        product = lax.dot_general(
            factor_ref[:, part],
            adapter_b_ref[...],
            (((0,), (0,)), ((), ())),
            preferred_element_type=jnp.float32,
        )
        merged = (base_ref[part, :].astype(jnp.float32) + product).astype(jnp.bfloat16)
        for column in range(columns // BLOCK):
            tile = merged[:, column * BLOCK : (column + 1) * BLOCK].astype(jnp.float32)
            scale = jnp.max(jnp.abs(tile), axis=(0, 1), keepdims=True) + 1e-06
            own[part, column * BLOCK : (column + 1) * BLOCK] = (tile / scale).astype(jnp.bfloat16)
            spread = jnp.where((lane % blocks == block) & (line == column), scale, spread)
        return spread

    z_end, x_end = sixteen(rows * 31 // 40), sixteen(rows * 3 // 5)
    cut = sixteen(rows * 2 // 5)
    z_pieces = ((0, cut), (cut, z_end))
    x_pieces = ((0, cut), (cut, x_end))
    yx_piece, yz_piece = (0, rows - x_end), (0, rows - z_end)

    def window(ref, piece, side):
        low, high = piece
        start = pl.multiple_of(low + side * (rows - high - low), 16)
        return ref.at[pl.ds(start, high - low)]

    def copy(source, plane, column, piece, side, send, recv, device):
        target = gathered.at[plane * 2 + column]
        source = target if source is None else source
        return pltpu.make_async_remote_copy(
            src_ref=window(source, piece, side),
            dst_ref=window(target, piece, side),
            send_sem=send,
            recv_sem=recv,
            device_id=device,
        )

    def z_copy(plane, piece, way, source=None):
        return copy(
            source,
            plane,
            x,
            z_pieces[piece],
            group,
            z_send.at[(way + 1) // 2, plane, piece],
            z_recv.at[plane, piece],
            {"replica": lax.rem(me + 2 * way + count, count)},
        )

    def x_copy(plane, piece, column, source=None):
        return copy(
            source,
            plane,
            column,
            x_pieces[piece],
            group,
            x_send.at[plane, piece],
            x_recv.at[plane, piece],
            {"replica": z * 2 + 1 - x},
        )

    def y_copy(plane, column, which, side):
        return copy(
            None,
            plane,
            column,
            (yx_piece, yz_piece)[which],
            side,
            y_send.at[which, plane],
            y_recv.at[which, plane],
            {"groups": 1 - group},
        )

    def scale_copy(step):
        return pltpu.make_async_remote_copy(
            src_ref=own_scales,
            dst_ref=scales_all.at[me],
            send_sem=scale_send.at[step],
            recv_sem=scale_recv.at[step],
            device_id={"replica": lax.rem(me + step, count)},
        )

    def attend(row, head):
        first = head * per_group
        query = jnp.concatenate(
            [
                queries_ref[row : row + 1, (first + i) * HD : (first + i + 1) * HD].astype(
                    jnp.float32
                )
                for i in range(per_group)
            ],
            axis=0,
        )
        wide = slice(head * HD, (head + 1) * HD)
        scaling = 1.0 / HD**0.5
        scores = (
            lax.dot_general(
                query.astype(jnp.bfloat16),
                keys[row, :, wide],
                (((1,), (1,)), ((), ())),
                preferred_element_type=jnp.float32,
            )
            * scaling
        )
        slot = lax.broadcasted_iota(jnp.int32, scores.shape, 1)
        scores = jnp.where(slot < lengths_ref[row], scores, -jnp.inf)
        new_key = new_keys_ref[row : row + 1, wide].astype(jnp.float32)
        own_score = jnp.sum(query * new_key, axis=1, keepdims=True) * scaling
        highest = jnp.maximum(jnp.max(scores, axis=1, keepdims=True), own_score)
        raised = jnp.exp(scores - highest)
        own_raised = jnp.exp(own_score - highest)
        totals = jnp.sum(raised, axis=1, keepdims=True) + own_raised
        weights = (raised / totals).astype(jnp.bfloat16)
        own_weight = (own_raised / totals).astype(jnp.bfloat16).astype(jnp.float32)
        mixed = jnp.dot(weights, values[row, :, wide], preferred_element_type=jnp.float32)
        new_value = new_values_ref[row : row + 1, wide].astype(jnp.float32)
        return mixed + own_weight * new_value

    first = -(-cut // BLOCK)
    spread = jnp.zeros(own_scales.shape, jnp.float32)
    for piece, steps in enumerate((range(first), range(first, blocks))):
        for step in steps:
            spread = scale_block(step, spread)
        if piece == 0:
            pl.semaphore_wait(barrier, count)

        @pl.when(z < depth - 1)
        def _():
            z_copy(z, piece, 1, own).start()

        @pl.when(z > 0)
        def _():
            z_copy(z, piece, -1, own).start()

        x_copy(z, piece, x, own).start()
    own_scales[...] = spread
    for step in range(1, count):
        scale_copy(step).start()
    own_out = pltpu.make_async_copy(own, gathered.at[me], local_sem.at[2])
    own_out.start()
    scales_out = pltpu.make_async_copy(own_scales, scales_all.at[me], local_sem.at[3])
    scales_out.start()

    def z_step(plane, piece, way):
        z_copy(plane, piece, way).wait_recv()

        @pl.when((z + way >= 0) & (z + way < depth))
        def _():
            z_copy(plane, piece, way).start()

        x_copy(plane, piece, x).start()
        if piece == 0:
            y_copy(plane, x, 1, group).start()

    def x_step(plane, piece):
        x_copy(plane, piece, 1 - x).wait_recv()
        if piece == 0:
            y_copy(plane, 1 - x, 0, group).start()

    keys_in.wait()
    values_in.wait()
    heads = kv_heads * per_group

    def attend_row(row):
        tall = jnp.concatenate([attend(row, head) for head in range(kv_heads)], axis=0)
        attended[row * heads : (row + 1) * heads, :] = tall.astype(jnp.bfloat16)

    attend_row(0)
    hand = pltpu.make_async_remote_copy(
        src_ref=attended,
        dst_ref=handed,
        send_sem=hand_sem.at[0],
        recv_sem=hand_sem.at[1],
        device_id={"replica": lax.rem(me + 1, count)},
    )
    for step in range(1, depth + 1):
        if step == 2:
            for row in range(1, row_count):
                attend_row(row)
            hand.start()
        for piece in range(2):
            if step < depth:

                @pl.when(z - step >= 0)
                def _():
                    z_step(z - step, piece, 1)

                @pl.when(z + step < depth)
                def _():
                    z_step(z + step, piece, -1)

            if step == 1:
                x_step(z, piece)
            else:

                @pl.when(z - step + 1 >= 0)
                def _():
                    x_step(z - step + 1, piece)

                @pl.when(z + step - 1 < depth)
                def _():
                    x_step(z + step - 1, piece)

    own_out.wait()
    scales_out.wait()
    hand.wait()
    for step in range(1, count):
        scale_copy(step).wait()
    for plane in range(depth):
        for piece in range(2):

            @pl.when((plane <= z) & (z < depth - 1))
            def _():
                z_copy(plane, piece, 1).wait_send()

            @pl.when((plane >= z) & (z > 0))
            def _():
                z_copy(plane, piece, -1).wait_send()

            x_copy(plane, piece, x).wait_send()
        y_copy(plane, 1 - x, 0, group).wait_send()
        y_copy(plane, 1 - x, 0, 1 - group).wait_recv()

        @pl.when(z != plane)
        def _():
            y_copy(plane, x, 1, group).wait_send()
            y_copy(plane, x, 1, 1 - group).wait_recv()


def place_kernel(
    owners_ref, scales_ref, handed_ref, gathered, placed, scales, rows_out, held, in_sems, out_sems
):
    count, rows, _ = gathered.shape
    fetches = [
        pltpu.make_async_copy(gathered.at[owners_ref[slot]], held.at[slot], in_sems.at[slot])
        for slot in range(count)
    ]
    copies = [
        pltpu.make_async_copy(
            held.at[slot], placed.at[pl.ds(slot * rows, rows)], out_sems.at[slot]
        )
        for slot in range(count)
    ]
    for moving in fetches:
        moving.start()
    for fetch, moving in zip(fetches, copies):
        fetch.wait()
        moving.start()
    blocks = scales.shape[1] // count
    lane = lax.broadcasted_iota(jnp.int32, scales_ref.shape[1:], 1)
    spread = jnp.zeros(scales_ref.shape[1:], jnp.float32)
    for slot in range(count):
        spread = jnp.where(lane // blocks == slot, scales_ref[owners_ref[slot]], spread)
    scales[...] = spread[: scales.shape[0], : scales.shape[1]]
    tall = handed_ref[...].astype(jnp.float32)
    row_count = rows_out.shape[0]
    heads = tall.shape[0] // row_count
    for row in range(row_count):
        rows_out[row : row + 1, :] = jnp.concatenate(
            [tall[row * heads + head : row * heads + head + 1] for head in range(heads)], axis=1
        ).astype(jnp.bfloat16)
    for moving in copies:
        moving.wait()


def on_plane(
    queries,
    new_keys,
    new_values,
    key_cache,
    value_cache,
    lengths,
    base_held,
    adapter_a,
    adapter_b,
    owners,
):
    replicas = lax.axis_size("replica")
    depth = replicas // 2
    rows, columns = base_held.shape
    row_count = queries.shape[0]
    heads = row_count * queries.shape[1] // HD
    vmem = pl.BlockSpec(memory_space=pltpu.VMEM)
    smem = pl.BlockSpec(memory_space=pltpu.SMEM)
    anywhere = pl.BlockSpec(memory_space=pl.ANY)
    gathered, scales_all, handed = pl.pallas_call(
        gather_kernel,
        out_shape=(
            jax.ShapeDtypeStruct((replicas, rows, columns), jnp.bfloat16),
            jax.ShapeDtypeStruct((replicas, 8, 128), jnp.float32),
            jax.ShapeDtypeStruct((heads, HD), jnp.bfloat16),
        ),
        in_specs=[vmem, vmem, vmem, smem, vmem, vmem, vmem, anywhere, anywhere],
        out_specs=(anywhere, anywhere, anywhere),
        scratch_shapes=[
            pltpu.VMEM((rows, columns), jnp.bfloat16),
            pltpu.VMEM((8, 128), jnp.float32),
            pltpu.VMEM((heads, HD), jnp.bfloat16),
            pltpu.VMEM(key_cache.shape, jnp.bfloat16),
            pltpu.VMEM(value_cache.shape, jnp.bfloat16),
            pltpu.SemaphoreType.DMA((4,)),
            pltpu.SemaphoreType.DMA((2, depth, 2)),
            pltpu.SemaphoreType.DMA((depth, 2)),
            pltpu.SemaphoreType.DMA((depth, 2)),
            pltpu.SemaphoreType.DMA((depth, 2)),
            pltpu.SemaphoreType.DMA((2, depth)),
            pltpu.SemaphoreType.DMA((2, depth)),
            pltpu.SemaphoreType.DMA((replicas,)),
            pltpu.SemaphoreType.DMA((replicas,)),
            pltpu.SemaphoreType.DMA((2,)),
        ],
        compiler_params=pltpu.CompilerParams(
            collective_id=0, has_side_effects=True, vmem_limit_bytes=60 * 2**20
        ),
        name="gather",
    )(
        queries,
        new_keys,
        new_values,
        lengths,
        base_held,
        adapter_a.T,
        adapter_b,
        key_cache,
        value_cache,
    )
    block_values, scales, handed_rows = pl.pallas_call(
        place_kernel,
        out_shape=(
            jax.ShapeDtypeStruct((replicas * rows, columns), jnp.bfloat16),
            jax.ShapeDtypeStruct((columns // BLOCK, replicas * rows // BLOCK), jnp.float32),
            jax.ShapeDtypeStruct(queries.shape, jnp.bfloat16),
        ),
        in_specs=[smem, vmem, vmem, anywhere],
        out_specs=(anywhere, vmem, vmem),
        scratch_shapes=[
            pltpu.VMEM((replicas, rows, columns), jnp.bfloat16),
            pltpu.SemaphoreType.DMA((replicas,)),
            pltpu.SemaphoreType.DMA((replicas,)),
        ],
        compiler_params=pltpu.CompilerParams(vmem_limit_bytes=60 * 2**20),
        name="place",
    )(owners, scales_all, handed, gathered)
    return (handed_rows, block_values, scales.T)


def solution(mesh):
    shape = dict(mesh.shape)
    relay = shape["groups"] == 2 and shape["replica"] % 2 == 0

    def either(*operands):
        rows, columns = operands[6].shape
        blocks = shape["replica"] * rows // BLOCK
        if relay and shape["replica"] <= 16 and rows % BLOCK == 0 and blocks <= 128 and columns <= 8 * BLOCK:
            return on_plane(*operands)
        return on_device(*operands)

    in_specs = (
        P(("groups", "replica"), "tensor"),
        P(("groups", "replica"), "tensor"),
        P(("groups", "replica"), "tensor"),
        P(("groups", "replica"), None, "tensor"),
        P(("groups", "replica"), None, "tensor"),
        P(("groups", "replica")),
        P("replica", "tensor"),
        P("replica", None),
        P(None, "tensor"),
        P(),
    )
    out_specs = (P(("groups", "replica"), "tensor"), P("groups", "tensor"), P("groups", "tensor"))
    return jax.shard_map(
        either, mesh=mesh, in_specs=in_specs, out_specs=out_specs, check_vma=False
    )
```

```python
import jax
import jax.numpy as jnp
from jax import lax
from jax.experimental import pallas as pl
from jax.experimental.pallas import tpu as pltpu
from jax.sharding import PartitionSpec as P

HD = 128
BLOCK = 128


def from_behind(value, axis, steps):
    count = lax.axis_size(axis)
    pairs = [(source, (source + steps) % count) for source in range(count)]
    return lax.ppermute(value, axis, pairs)


def merge_rows(base_rows, factor_rows, adapter_b):
    return (
        base_rows.astype(jnp.float32)
        + jnp.dot(factor_rows, adapter_b, preferred_element_type=jnp.float32)
    ).astype(jnp.bfloat16)


def on_device(
    queries,
    new_keys,
    new_values,
    key_cache,
    value_cache,
    lengths,
    base_held,
    adapter_a,
    adapter_b,
    owners,
):
    replicas = lax.axis_size("replica")
    slice_rows, columns = base_held.shape
    merged = merge_rows(base_held, adapter_a, adapter_b)
    everything = lax.all_gather(merged, "replica", axis=0, tiled=True)
    assembled = jnp.take(everything.reshape(replicas, slice_rows, columns), owners, axis=0).reshape(
        replicas * slice_rows, columns
    )
    total_rows = assembled.shape[0]
    tiled = assembled.astype(jnp.float32).reshape(
        total_rows // BLOCK, BLOCK, columns // BLOCK, BLOCK
    )
    block_scales = jnp.max(jnp.abs(tiled), axis=(1, 3)) + 1e-06
    block_values = (
        (tiled / block_scales[:, None, :, None]).reshape(total_rows, columns).astype(jnp.bfloat16)
    )
    row_count = queries.shape[0]
    slot_count = key_cache.shape[1]
    kv_heads = key_cache.shape[2] // HD
    per_group = queries.shape[1] // HD // kv_heads
    scaling = 1.0 / HD**0.5
    query_heads = queries.reshape(row_count, kv_heads, per_group, HD)
    cached_keys = key_cache.reshape(row_count, slot_count, kv_heads, HD)
    cached_values = value_cache.reshape(row_count, slot_count, kv_heads, HD)
    scores = (
        jnp.einsum("rgqd,rlgd->rgql", query_heads, cached_keys, preferred_element_type=jnp.float32)
        * scaling
    )
    usable = jnp.arange(slot_count)[None, None, None, :] < lengths[:, None, None, None]
    scores = jnp.where(usable, scores, -jnp.inf)
    own_score = (
        jnp.einsum(
            "rgqd,rgd->rgq",
            query_heads,
            new_keys.reshape(row_count, kv_heads, HD),
            preferred_element_type=jnp.float32,
        )
        * scaling
    )
    highest = jnp.maximum(jnp.max(scores, axis=-1), own_score)
    raised = jnp.exp(scores - highest[..., None])
    own_raised = jnp.exp(own_score - highest)
    totals = jnp.sum(raised, axis=-1) + own_raised
    weights = (raised / totals[..., None]).astype(jnp.bfloat16)
    own_weight = (own_raised / totals).astype(jnp.bfloat16)
    mixed = jnp.einsum(
        "rgql,rlgd->rgqd", weights, cached_values, preferred_element_type=jnp.float32
    )
    mixed = mixed + own_weight.astype(jnp.float32)[..., None] * new_values.reshape(
        row_count, kv_heads, 1, HD
    ).astype(jnp.float32)
    attended = mixed.reshape(row_count, kv_heads * per_group * HD).astype(jnp.bfloat16)
    handed_rows = from_behind(attended, "replica", 1)
    return (handed_rows, block_values, block_scales)


def gather_kernel(
    queries_hbm,
    new_keys_hbm,
    new_values_hbm,
    lengths_hbm,
    base_hbm,
    factor_hbm,
    adapter_b_hbm,
    keys_hbm,
    values_hbm,
    gathered,
    scales_all,
    handed,
    own,
    own_scales,
    attended,
    keys,
    values,
    queries_ref,
    new_keys_ref,
    new_values_ref,
    lengths_ref,
    base_ref,
    factor_ref,
    adapter_b_ref,
    local_sem,
    z_send,
    z_recv,
    x_send,
    x_recv,
    y_send,
    y_recv,
    scale_send,
    scale_recv,
    hand_sem,
):
    group = lax.axis_index("groups")
    me = lax.axis_index("replica")
    count = lax.axis_size("replica")
    depth = count // 2
    z = me // 2
    x = me % 2
    rows, columns = base_ref.shape
    row_count, slot_count, _ = keys.shape
    kv_heads = columns // HD
    per_group = queries_ref.shape[1] // HD // kv_heads

    barrier = pltpu.get_barrier_semaphore()
    for step in range(1, count):
        pl.semaphore_signal(
            barrier, inc=1, device_id={"replica": lax.rem(me + step, count)}
        )
    pl.semaphore_signal(barrier, inc=1, device_id={"groups": 1 - group})

    places = (
        (base_hbm, base_ref),
        (factor_hbm, factor_ref),
        (adapter_b_hbm, adapter_b_ref),
        (keys_hbm, keys),
        (values_hbm, values),
        (queries_hbm, queries_ref),
        (new_keys_hbm, new_keys_ref),
        (new_values_hbm, new_values_ref),
        (lengths_hbm, lengths_ref),
    )
    arriving = [
        pltpu.make_async_copy(source, target, local_sem.at[2 + number])
        for number, (source, target) in enumerate(places)
    ]
    for moving in arriving:
        moving.start()
    for moving in arriving[:3]:
        moving.wait()
    lane = lax.broadcasted_iota(jnp.int32, own_scales.shape, 1)
    line = lax.broadcasted_iota(jnp.int32, own_scales.shape, 0)
    blocks = rows // BLOCK

    def scale_block(step, spread):
        block = step + group * (blocks - 1 - 2 * step)
        part = pl.ds(pl.multiple_of(block * BLOCK, BLOCK), BLOCK)
        product = lax.dot_general(
            factor_ref[:, part],
            adapter_b_ref[...],
            (((0,), (0,)), ((), ())),
            preferred_element_type=jnp.float32,
        )
        merged = (base_ref[part, :].astype(jnp.float32) + product).astype(jnp.bfloat16)
        for column in range(columns // BLOCK):
            tile = merged[:, column * BLOCK : (column + 1) * BLOCK].astype(jnp.float32)
            scale = jnp.max(jnp.abs(tile), axis=(0, 1), keepdims=True) + 1e-06
            own[part, column * BLOCK : (column + 1) * BLOCK] = (tile / scale).astype(jnp.bfloat16)
            spread = jnp.where((lane % blocks == block) & (line == column), scale, spread)
        return spread

    z_pieces = blocks - 1
    x_pieces = max(blocks - blocks // 2, 1)
    yx_pieces, yz_pieces = blocks - x_pieces, 1

    def window(ref, piece, side):
        block = piece + side * (blocks - 1 - 2 * piece)
        return ref.at[pl.ds(pl.multiple_of(block * BLOCK, BLOCK), BLOCK)]

    def copy(source, plane, column, piece, side, send, recv, device):
        target = gathered.at[plane * 2 + column]
        source = target if source is None else source
        return pltpu.make_async_remote_copy(
            src_ref=window(source, piece, side),
            dst_ref=window(target, piece, side),
            send_sem=send,
            recv_sem=recv,
            device_id=device,
        )

    def z_copy(plane, piece, way, source=None):
        return copy(
            source,
            plane,
            x,
            piece,
            group,
            z_send.at[(way + 1) // 2, plane, piece],
            z_recv.at[plane, piece],
            {"replica": lax.rem(me + 2 * way + count, count)},
        )

    def x_copy(plane, piece, column, source=None):
        return copy(
            source,
            plane,
            column,
            piece,
            group,
            x_send.at[plane, piece],
            x_recv.at[plane, piece],
            {"replica": z * 2 + 1 - x},
        )

    def y_copy(plane, column, piece, side):
        slot = jnp.where(column == x, x_pieces, 0) + piece
        return copy(
            None,
            plane,
            column,
            piece,
            side,
            y_send.at[plane, slot],
            y_recv.at[plane, slot],
            {"groups": 1 - group},
        )

    def scale_copy(step):
        return pltpu.make_async_remote_copy(
            src_ref=own_scales,
            dst_ref=scales_all.at[me],
            send_sem=scale_send.at[step],
            recv_sem=scale_recv.at[step],
            device_id={"replica": lax.rem(me + step, count)},
        )

    def attend(row, head):
        first = head * per_group
        query = jnp.concatenate(
            [
                queries_ref[row : row + 1, (first + i) * HD : (first + i + 1) * HD].astype(
                    jnp.float32
                )
                for i in range(per_group)
            ],
            axis=0,
        )
        wide = slice(head * HD, (head + 1) * HD)
        scaling = 1.0 / HD**0.5
        scores = (
            lax.dot_general(
                query.astype(jnp.bfloat16),
                keys[row, :, wide],
                (((1,), (1,)), ((), ())),
                preferred_element_type=jnp.float32,
            )
            * scaling
        )
        slot = lax.broadcasted_iota(jnp.int32, scores.shape, 1)
        scores = jnp.where(slot < lengths_ref[row], scores, -jnp.inf)
        new_key = new_keys_ref[row : row + 1, wide].astype(jnp.float32)
        own_score = jnp.sum(query * new_key, axis=1, keepdims=True) * scaling
        highest = jnp.maximum(jnp.max(scores, axis=1, keepdims=True), own_score)
        raised = jnp.exp(scores - highest)
        own_raised = jnp.exp(own_score - highest)
        totals = jnp.sum(raised, axis=1, keepdims=True) + own_raised
        weights = (raised / totals).astype(jnp.bfloat16)
        own_weight = (own_raised / totals).astype(jnp.bfloat16).astype(jnp.float32)
        mixed = jnp.dot(weights, values[row, :, wide], preferred_element_type=jnp.float32)
        new_value = new_values_ref[row : row + 1, wide].astype(jnp.float32)
        return mixed + own_weight * new_value

    spread = jnp.zeros(own_scales.shape, jnp.float32)
    for piece in range(blocks):
        spread = scale_block(piece, spread)
        if piece == 0:
            pl.semaphore_wait(barrier, count)
        if piece < z_pieces:

            @pl.when(z < depth - 1)
            def _():
                z_copy(z, piece, 1, own).start()

            @pl.when(z > 0)
            def _():
                z_copy(z, piece, -1, own).start()

        if piece < x_pieces:
            x_copy(z, piece, x, own).start()
    own_scales[...] = spread
    for step in range(1, count):
        scale_copy(step).start()
    own_out = pltpu.make_async_copy(own, gathered.at[me], local_sem.at[0])
    own_out.start()
    scales_out = pltpu.make_async_copy(own_scales, scales_all.at[me], local_sem.at[1])
    scales_out.start()

    def z_step(plane, piece, way):
        z_copy(plane, piece, way).wait_recv()

        @pl.when((z + way >= 0) & (z + way < depth))
        def _():
            z_copy(plane, piece, way).start()

        if piece < x_pieces:
            x_copy(plane, piece, x).start()
        if piece < yz_pieces:
            y_copy(plane, x, piece, group).start()

    def x_step(plane, piece):
        x_copy(plane, piece, 1 - x).wait_recv()
        if piece < yx_pieces:
            y_copy(plane, 1 - x, piece, group).start()

    for moving in arriving[3:]:
        moving.wait()
    heads = kv_heads * per_group

    def attend_row(row):
        tall = jnp.concatenate([attend(row, head) for head in range(kv_heads)], axis=0)
        attended[row * heads : (row + 1) * heads, :] = tall.astype(jnp.bfloat16)

    attend_row(0)
    hand = pltpu.make_async_remote_copy(
        src_ref=attended,
        dst_ref=handed,
        send_sem=hand_sem.at[0],
        recv_sem=hand_sem.at[1],
        device_id={"replica": lax.rem(me + 1, count)},
    )
    for step in range(1, depth + 1):
        if step == 2:
            for row in range(1, row_count):
                attend_row(row)
            hand.start()
        for piece in range(z_pieces):
            if step < depth:

                @pl.when(z - step >= 0)
                def _():
                    z_step(z - step, piece, 1)

                @pl.when(z + step < depth)
                def _():
                    z_step(z + step, piece, -1)

            if piece < x_pieces:
                if step == 1:
                    x_step(z, piece)
                else:

                    @pl.when(z - step + 1 >= 0)
                    def _():
                        x_step(z - step + 1, piece)

                    @pl.when(z + step - 1 < depth)
                    def _():
                        x_step(z + step - 1, piece)

    own_out.wait()
    scales_out.wait()
    hand.wait()
    for step in range(1, count):
        scale_copy(step).wait()
    for plane in range(depth):
        for piece in range(z_pieces):

            @pl.when((plane <= z) & (z < depth - 1))
            def _():
                z_copy(plane, piece, 1).wait_send()

            @pl.when((plane >= z) & (z > 0))
            def _():
                z_copy(plane, piece, -1).wait_send()

        for piece in range(x_pieces):
            x_copy(plane, piece, x).wait_send()
        for piece in range(yx_pieces):
            y_copy(plane, 1 - x, piece, group).wait_send()
            y_copy(plane, 1 - x, piece, 1 - group).wait_recv()

        @pl.when(z != plane)
        def _():
            for piece in range(yz_pieces):
                y_copy(plane, x, piece, group).wait_send()
                y_copy(plane, x, piece, 1 - group).wait_recv()


def place_kernel(
    owners_ref, scales_ref, handed_ref, gathered, placed, scales, rows_out, held, in_sems, out_sems
):
    count, rows, _ = gathered.shape
    fetches = [
        pltpu.make_async_copy(gathered.at[owners_ref[slot]], held.at[slot], in_sems.at[slot])
        for slot in range(count)
    ]
    copies = [
        pltpu.make_async_copy(
            held.at[slot], placed.at[pl.ds(slot * rows, rows)], out_sems.at[slot]
        )
        for slot in range(count)
    ]
    for moving in fetches:
        moving.start()
    for fetch, moving in zip(fetches, copies):
        fetch.wait()
        moving.start()
    blocks = scales.shape[1] // count
    lane = lax.broadcasted_iota(jnp.int32, scales_ref.shape[1:], 1)
    spread = jnp.zeros(scales_ref.shape[1:], jnp.float32)
    for slot in range(count):
        spread = jnp.where(lane // blocks == slot, scales_ref[owners_ref[slot]], spread)
    scales[...] = spread[: scales.shape[0], : scales.shape[1]]
    tall = handed_ref[...].astype(jnp.float32)
    row_count = rows_out.shape[0]
    heads = tall.shape[0] // row_count
    for row in range(row_count):
        rows_out[row : row + 1, :] = jnp.concatenate(
            [tall[row * heads + head : row * heads + head + 1] for head in range(heads)], axis=1
        ).astype(jnp.bfloat16)
    for moving in copies:
        moving.wait()


def on_plane(
    queries,
    new_keys,
    new_values,
    key_cache,
    value_cache,
    lengths,
    base_held,
    adapter_a,
    adapter_b,
    owners,
):
    replicas = lax.axis_size("replica")
    depth = replicas // 2
    rows, columns = base_held.shape
    blocks = rows // BLOCK
    row_count = queries.shape[0]
    heads = row_count * queries.shape[1] // HD
    vmem = pl.BlockSpec(memory_space=pltpu.VMEM)
    smem = pl.BlockSpec(memory_space=pltpu.SMEM)
    anywhere = pl.BlockSpec(memory_space=pl.ANY)
    hbm = pl.BlockSpec(memory_space=pltpu.HBM)
    gathered, scales_all, handed = pl.pallas_call(
        gather_kernel,
        out_shape=(
            jax.ShapeDtypeStruct((replicas, rows, columns), jnp.bfloat16),
            jax.ShapeDtypeStruct((replicas, 8, 128), jnp.float32),
            jax.ShapeDtypeStruct((heads, HD), jnp.bfloat16),
        ),
        in_specs=[hbm, hbm, hbm, hbm, hbm, hbm, hbm, hbm, hbm],
        out_specs=(anywhere, anywhere, anywhere),
        scratch_shapes=[
            pltpu.VMEM((rows, columns), jnp.bfloat16),
            pltpu.VMEM((8, 128), jnp.float32),
            pltpu.VMEM((heads, HD), jnp.bfloat16),
            pltpu.VMEM(key_cache.shape, jnp.bfloat16),
            pltpu.VMEM(value_cache.shape, jnp.bfloat16),
            pltpu.VMEM(queries.shape, jnp.bfloat16),
            pltpu.VMEM(new_keys.shape, jnp.bfloat16),
            pltpu.VMEM(new_values.shape, jnp.bfloat16),
            pltpu.SMEM(lengths.shape, jnp.int32),
            pltpu.VMEM(base_held.shape, jnp.bfloat16),
            pltpu.VMEM(adapter_a.shape[::-1], jnp.bfloat16),
            pltpu.VMEM(adapter_b.shape, jnp.bfloat16),
            pltpu.SemaphoreType.DMA((11,)),
            pltpu.SemaphoreType.DMA((2, depth, blocks)),
            pltpu.SemaphoreType.DMA((depth, blocks)),
            pltpu.SemaphoreType.DMA((depth, blocks)),
            pltpu.SemaphoreType.DMA((depth, blocks)),
            pltpu.SemaphoreType.DMA((depth, blocks)),
            pltpu.SemaphoreType.DMA((depth, blocks)),
            pltpu.SemaphoreType.DMA((replicas,)),
            pltpu.SemaphoreType.DMA((replicas,)),
            pltpu.SemaphoreType.DMA((2,)),
        ],
        compiler_params=pltpu.CompilerParams(
            collective_id=0, has_side_effects=True, vmem_limit_bytes=60 * 2**20
        ),
        name="gather",
    )(
        queries,
        new_keys,
        new_values,
        lengths,
        base_held,
        adapter_a.T,
        adapter_b,
        key_cache,
        value_cache,
    )
    block_values, scales, handed_rows = pl.pallas_call(
        place_kernel,
        out_shape=(
            jax.ShapeDtypeStruct((replicas * rows, columns), jnp.bfloat16),
            jax.ShapeDtypeStruct((columns // BLOCK, replicas * rows // BLOCK), jnp.float32),
            jax.ShapeDtypeStruct(queries.shape, jnp.bfloat16),
        ),
        in_specs=[smem, vmem, vmem, anywhere],
        out_specs=(anywhere, vmem, vmem),
        scratch_shapes=[
            pltpu.VMEM((replicas, rows, columns), jnp.bfloat16),
            pltpu.SemaphoreType.DMA((replicas,)),
            pltpu.SemaphoreType.DMA((replicas,)),
        ],
        compiler_params=pltpu.CompilerParams(vmem_limit_bytes=60 * 2**20),
        name="place",
    )(owners, scales_all, handed, gathered)
    return (handed_rows, block_values, scales.T)


def solution(mesh):
    shape = dict(mesh.shape)
    relay = shape["groups"] == 2 and shape["replica"] % 2 == 0

    def either(*operands):
        rows, columns = operands[6].shape
        blocks = shape["replica"] * rows // BLOCK
        if relay and shape["replica"] <= 16 and rows % BLOCK == 0 and rows > 2 * BLOCK and blocks <= 128 and columns <= 8 * BLOCK:
            return on_plane(*operands)
        return on_device(*operands)

    in_specs = (
        P(("groups", "replica"), "tensor"),
        P(("groups", "replica"), "tensor"),
        P(("groups", "replica"), "tensor"),
        P(("groups", "replica"), None, "tensor"),
        P(("groups", "replica"), None, "tensor"),
        P(("groups", "replica")),
        P("replica", "tensor"),
        P("replica", None),
        P(None, "tensor"),
        P(),
    )
    out_specs = (P(("groups", "replica"), "tensor"), P("groups", "tensor"), P("groups", "tensor"))
    return jax.shard_map(
        either, mesh=mesh, in_specs=in_specs, out_specs=out_specs, check_vma=False
    )
```
